256 devices in a mesh: tm: 8 (over x, core), seq: 32 (over y, z).
Axes of the slice: x: 4, y: 4, z: 8, core: 2. Of those that a mesh axis runs over, the one named last changes fastest.
Arguments:
- projected: bfloat16 [8, 4096, 3, 4096], P('tm', 'seq'), may hold values from -16 to 16
- scale_table: float32 [8, 3, 32], replicated, may hold values from 0.8 to 1.25
- group_index: int32 [8], P('tm'), may hold values from 0 to 7
- timesteps: int32 [8], P('tm'), may hold values from 1 to 999, as said below
- time_weight: bfloat16 [256, 2, 4096], replicated, may hold values from -0.375 to 0.375
- head_weight: bfloat16 [64, 4096], replicated, may hold values from -0.09375 to 0.09375
- start_latent: float32 [2048, 128], P('seq'), may hold values from -3 to 3
Outputs:
- latents: float32 [8, 2048, 128], P('tm', 'seq')
The draws below stay inside these ranges and needn't reach their ends.
Inputs may be any that keep to these rules, and one draw needn't show every extreme that they name: `timesteps`: strictly decreasing along the steps.
All inputs are finite; a program needn't handle non-finite values.
Results may differ from the reference program's by a relative error of at most 0.0026.
Values may be sent and summed in bfloat16 or wider, within the bound.
A program may use at most 64 MiB of HBM per device.

```python
import math
import jax
import jax.numpy as jnp
from jax import lax

HEADS = 32
HEAD_SIZE = 128
LAT = 64
FREQ = 256
GROUPS = 8
WIDTH = 4096
TOKENS = 4096
STEPS = 8


def draw_projected(key, part):
    key = jax.random.fold_in(key, 11)
    key_base = jax.random.fold_in(key, 0)
    array_shape = (STEPS, TOKENS, 3, WIDTH)
    drawn_codes = jnp.clip(jax.random.normal(key_base, array_shape, jnp.float32), -6.0, 6.0)
    return drawn_codes.astype(jnp.bfloat16)


def draw_timesteps(key, part):
    key = jax.random.fold_in(key, 23)
    key_first, key_spacing = jax.random.split(key)
    opening = jax.random.randint(key_first, (), 950, 1000)
    spacing = jax.random.randint(key_spacing, (STEPS,), 10, 900 // STEPS + 1)
    return (opening - jnp.cumsum(spacing) + spacing).astype(jnp.int32)


def with_ends(values, key, low, largest):
    dims = values.shape
    spot = [jax.random.randint(jax.random.fold_in(key, axis), (), 0, dims[axis]) for axis in range(len(dims))]
    values = values.at[tuple(spot)].set(low)
    longest = dims.index(max(dims))
    spot[longest] = (spot[longest] + 1) % dims[longest]
    return values.at[tuple(spot)].set(largest)


def block_scale(rng, dims, cuts, least, high):
    gain = 1.0
    for position, blocks in cuts:
        steps = jax.random.uniform(jax.random.fold_in(jax.random.fold_in(rng, 6), position), (blocks,), jnp.float32, least / len(cuts), high / len(cuts))
        gain = gain * jnp.repeat(jnp.exp(steps), dims[position] // blocks).reshape((-1,) + (1,) * (len(dims) - 1 - position))
    return gain


def scatter_about(key, dims, scale, limit, shards=(), kind=jnp.bfloat16):
    array = scale * jax.random.normal(key, dims, jnp.float32)
    if shards:
        array = array * block_scale(key, dims, shards, -0.22, 0.18)
    return jnp.clip(array, -limit, limit).astype(kind)


def setup_inputs(seed: int = 0) -> dict:
    seeds = jax.random.split(jax.random.key(seed), 8)
    projected = draw_projected(jax.random.fold_in(seeds[7], 71), 0)
    scale_table = jnp.clip(jnp.exp(jax.random.uniform(seeds[1], (GROUPS, 3, HEADS), jnp.float32, math.log(0.8), math.log(1.25))), 0.8, 1.25)
    group_index = with_ends(jax.random.randint(seeds[2], (STEPS,), 0, GROUPS), jax.random.fold_in(seeds[2], 1), 0, GROUPS - 1).astype(jnp.int32)
    timesteps = draw_timesteps(jax.random.fold_in(seeds[7], 71), 0)
    time_weight = scatter_about(seeds[4], (FREQ, 2, WIDTH), FREQ ** -0.5, 0.375)
    head_weight = scatter_about(seeds[5], (LAT, WIDTH), WIDTH ** -0.5, 0.09375)
    start_latent = scatter_about(seeds[6], (TOKENS // 2, 2 * LAT), 0.5, 3.0, ((0, 32),), jnp.float32)
    return {"projected": projected, "scale_table": scale_table, "group_index": group_index, "timesteps": timesteps, "time_weight": time_weight, "head_weight": head_weight, "start_latent": start_latent}


def sinusoid(times, freq_dim):
    half_freq = freq_dim // 2
    frequencies = jnp.power(jnp.float32(10000.0), -jnp.arange(half_freq, dtype=jnp.float32) / half_freq)
    angles = times.astype(jnp.float32)[:, None] * frequencies[None, :]
    return jnp.concatenate([jnp.cos(angles), jnp.sin(angles)], axis=1)

def modulate(outputs, shift_part, scale_part, center, inverse):
    return ((outputs.astype(jnp.float32) - center) * inverse * (1.0 + scale_part) + shift_part).astype(jnp.bfloat16)

def head_attention(operands):
    query_codes, key_codes, value_codes, factor, value_scale = operands
    scores = jnp.dot(query_codes, key_codes.T, preferred_element_type=jnp.float32) * factor
    row_max = lax.optimization_barrier(jnp.max(scores, axis=-1, keepdims=True))
    weights = jnp.exp(scores - row_max)
    row_sum = lax.optimization_barrier(jnp.sum(weights, axis=-1, keepdims=True))
    blended = jnp.dot(weights.astype(jnp.bfloat16), value_codes, preferred_element_type=jnp.float32)
    return (blended * (value_scale / row_sum)).astype(jnp.bfloat16)

def reference(projected, scale_table, group_index, timesteps, time_weight, head_weight, start_latent):
    later_times = jnp.concatenate([timesteps[1:], jnp.zeros((1,), jnp.int32)])
    step_size = (later_times - timesteps).astype(jnp.float32) / 1000.0
    embedded = sinusoid(timesteps, FREQ).astype(jnp.bfloat16)
    modulation = jnp.dot(embedded, time_weight.reshape(FREQ, 2 * WIDTH), preferred_element_type=jnp.float32)
    drift_list = []
    for step_index in range(STEPS):
        table_row = scale_table[group_index[step_index]]
        factor = table_row[0] * table_row[1] / math.sqrt(HEAD_SIZE)
        coded = projected[step_index].reshape(TOKENS, 3, HEADS, HEAD_SIZE)
        per_head = lax.map(head_attention, (coded[:, 0].transpose(1, 0, 2), coded[:, 1].transpose(1, 0, 2), coded[:, 2].transpose(1, 0, 2), factor, table_row[2]))
        attended = per_head.transpose(1, 0, 2).reshape(TOKENS, WIDTH)
        as_float = attended.astype(jnp.float32)
        center = lax.optimization_barrier(jnp.mean(as_float, axis=-1, keepdims=True))
        spread = lax.optimization_barrier(jnp.mean(jnp.square(as_float - center), axis=-1, keepdims=True))
        normed = modulate(attended, modulation[step_index, :WIDTH], modulation[step_index, WIDTH:], center, lax.rsqrt(spread + 1e-06))
        velocity = lax.dot_general(normed, head_weight, (((1,), (1,)), ((), ())), preferred_element_type=jnp.float32)
        drift_list.append(step_size[step_index] * velocity.reshape(TOKENS // 2, 2 * LAT))
    summed = jnp.cumsum(jnp.stack(drift_list), axis=0)
    return start_latent[None] + summed
```

```python
import functools
import math

import jax
import jax.numpy as jnp
import numpy as np
from jax import lax
from jax.experimental import pallas as pl
from jax.experimental.pallas import tpu as pltpu
from jax.sharding import PartitionSpec as P

MESH = pl.DeviceIdType.MESH
F32 = jnp.float32
BF16 = jnp.bfloat16

NY, NZ, TM = 4, 8, 8
SEQ = NY * NZ
TOK = 128
HEAD = 128
LAT = 64
KEYS = SEQ * TOK
WIDTH = SEQ * HEAD
FREQ = 256
ROWS = 256
KEY_CHUNK = 512
PACK = 72


def group_dz(g):
    odd = g % 2
    return (4 + odd * ((g + 1) // 2) - (1 - odd) * (g // 2)) % NZ


def group_dy(i):
    return (i + 1) % NY


def kernel(
    proj,
    scale_table,
    group_index,
    timesteps,
    freqs,
    time_weight,
    head_weight,
    start_latent,
    out,
    qbuf,
    kvbuf,
    ktbuf,
    sbuf,
    wblk,
    tw,
    hw,
    consts,
    pbuf,
    ybuf,
    zsend,
    zbuf,
    tsend,
    tbuf,
    later,
    lat,
    kv_send,
    kv_recv,
    q_send,
    q_recv,
    y_send,
    y_recv,
    z_send,
    z_recv,
    t_send,
    t_recv,
    misc,
):
    tm = lax.axis_index("tm")
    me = lax.axis_index("seq")
    my, mz = me // NZ, me % NZ

    def seq_at(dy, dz):
        return ((my + dy + NY) % NY) * NZ + (mz + dz + NZ) % NZ

    def peer(dy, dz):
        return (tm, seq_at(dy, dz))

    cols = pl.ds(pl.multiple_of(me * HEAD, HEAD), HEAD)
    own_codes = pltpu.make_async_copy(proj.at[1:3, :, cols], kvbuf.at[SEQ - 1], misc.at[0])
    own_query = pltpu.make_async_copy(proj.at[0, :, cols], qbuf.at[SEQ - 1], misc.at[1])
    get_tw = pltpu.make_async_copy(time_weight.at[:, :, cols], tw, misc.at[2])
    get_hw = pltpu.make_async_copy(head_weight.at[:, cols], hw, misc.at[3])
    own_codes.start()
    own_query.start()
    get_tw.start()
    get_hw.start()

    barrier = pltpu.get_barrier_semaphore()

    def greet(o, _):
        pl.semaphore_signal(barrier, inc=1, device_id=(tm, (me + o) % SEQ), device_id_type=MESH)
        return 0

    def greet_tm(o, _):
        pl.semaphore_signal(barrier, inc=1, device_id=((tm + o) % TM, me), device_id_type=MESH)
        return 0

    with jax.named_scope("barrier"):
        lax.fori_loop(1, SEQ, greet, 0)
        lax.fori_loop(1, TM, greet_tm, 0)
        pl.semaphore_wait(barrier, SEQ + TM - 2)

    def kv_copy(j):
        g, i = j // NY, j % NY
        to = seq_at(-group_dy(i), -group_dz(g))
        lanes = pl.ds(pl.multiple_of(to * HEAD, HEAD), HEAD)
        return pltpu.make_async_remote_copy(
            src_ref=proj.at[1:3, :, lanes],
            dst_ref=kvbuf.at[j],
            send_sem=kv_send.at[j],
            recv_sem=kv_recv.at[j],
            device_id=(tm, to),
            device_id_type=MESH,
        )

    def q_copy(j):
        g, i = j // NY, j % NY
        to = seq_at(-group_dy(i), -group_dz(g))
        lanes = pl.ds(pl.multiple_of(to * HEAD, HEAD), HEAD)
        return pltpu.make_async_remote_copy(
            src_ref=proj.at[0, :, lanes],
            dst_ref=qbuf.at[j],
            send_sem=q_send.at[j],
            recv_sem=q_recv.at[j],
            device_id=(tm, to),
            device_id_type=MESH,
        )

    def start_kv(j, _):
        kv_copy(j).start()
        return 0

    def start_q(j, _):
        q_copy(j).start()
        return 0

    with jax.named_scope("send"):
        lax.fori_loop(0, SEQ - 1, start_kv, 0)
        lax.fori_loop(0, SEQ - 1, start_q, 0)

    time_copy = pltpu.make_async_remote_copy(
        src_ref=later.at[0],
        dst_ref=later.at[1],
        send_sem=misc.at[4],
        recv_sem=misc.at[5],
        device_id=((tm + TM - 1) % TM, me),
        device_id_type=MESH,
    )
    time_now = jnp.full((8, 128), timesteps[0], jnp.int32).astype(F32)
    later[0] = time_now

    @pl.when(tm > 0)
    def _():
        time_copy.start()

    with jax.named_scope("constants"):
        lane = lax.broadcasted_iota(jnp.int32, (8, 128), 1)
        row = lax.broadcasted_iota(jnp.int32, (8, 128), 0)
        head_lane = lax.broadcasted_iota(jnp.int32, (8, SEQ), 1)
        group_row = lax.broadcasted_iota(jnp.int32, (8, SEQ), 0)
        chosen = (head_lane == me) & (group_row == group_index[0])

        def pick(k):
            kept = jnp.where(chosen, scale_table[k], 0.0)
            return jnp.sum(jnp.sum(kept, axis=1, keepdims=True), axis=0, keepdims=True)

        factor = pick(0) * pick(1) / math.sqrt(HEAD)
        score_scale = factor * math.log2(math.e)
        value_scale = pick(2)

        angles = time_now[0:1, 0:1] * freqs[...]
        wide_lane = lax.broadcasted_iota(jnp.int32, (8, 2 * FREQ), 1)
        wide_row = lax.broadcasted_iota(jnp.int32, (8, 2 * FREQ), 0)
        waves = jnp.where(wide_lane < FREQ, jnp.cos(angles), jnp.sin(angles))
        waves = jnp.where(wide_lane % 2 == wide_row, waves, 0.0).astype(BF16)
        get_tw.wait()
        get_hw.wait()
        modulation = jnp.dot(waves, tw[...].reshape(2 * FREQ, HEAD), preferred_element_type=F32)
        shift, scale = modulation[0:1], modulation[1:2]
        weight = hw[...].astype(F32)
        weight = jnp.concatenate([weight, weight], axis=0)
        scaled = (weight * (1.0 + scale)).T
        shifted = jnp.sum((weight * shift).T, axis=0, keepdims=True)
        high = scaled.astype(BF16)
        low = (scaled - high.astype(F32)).astype(BF16)
        left = lax.broadcasted_iota(jnp.int32, (HEAD, 128), 1) < LAT
        zero = jnp.zeros_like(high)
        wblk[0:HEAD, 0:128] = jnp.where(left, high, zero)
        wblk[0:HEAD, 128:256] = jnp.where(left, low, zero)
        wblk[HEAD : 2 * HEAD, 0:128] = jnp.where(left, zero, high)
        wblk[HEAD : 2 * HEAD, 128:256] = jnp.where(left, zero, low)
        summed = jnp.sum(high.astype(F32) + low.astype(F32), axis=0, keepdims=True)
        consts[...] = jnp.where(row == 2, summed, jnp.where(row == 3, shifted, 0.0))

    own_codes.wait()
    ktbuf[:, KEYS - TOK : KEYS] = kvbuf[SEQ - 1, 0].T

    def take_kv(j, _):
        kv_copy(j).wait_recv()
        ktbuf[:, pl.ds(pl.multiple_of(j * TOK, TOK), TOK)] = kvbuf[j, 0].T
        return 0

    with jax.named_scope("keys"):
        lax.fori_loop(0, SEQ - 1, take_kv, 0)

    def y_copy(g, i):
        return pltpu.make_async_remote_copy(
            src_ref=pbuf.at[g * NY + i],
            dst_ref=ybuf.at[g * NY + i],
            send_sem=y_send.at[g * NY + i],
            recv_sem=y_recv.at[g * NY + i],
            device_id=peer(group_dy(i), 0),
            device_id_type=MESH,
        )

    def z_copy(g):
        return pltpu.make_async_remote_copy(
            src_ref=zsend.at[g],
            dst_ref=zbuf.at[g],
            send_sem=z_send.at[g],
            recv_sem=z_recv.at[g],
            device_id=peer(0, group_dz(g)),
            device_id_type=MESH,
        )

    def join_y(g):
        total = pbuf[g * NY + NY - 1]
        for i in range(NY - 1):
            y_copy(g, i).wait_recv()
            total = total + ybuf[g * NY + i]
        zsend[g] = total

    keys_of = lambda c: slice(c * KEY_CHUNK, (c + 1) * KEY_CHUNK)
    chunks = KEYS // KEY_CHUNK
    ones = jnp.ones((KEY_CHUNK, 128), BF16)
    stat_row = lax.broadcasted_iota(jnp.int32, (16, 3 * HEAD), 0)
    stat_lane = lax.broadcasted_iota(jnp.int32, (16, 3 * HEAD), 1)
    picker = jnp.where(
        ((stat_row == 0) & (stat_lane < HEAD)) | ((stat_row == 1) & (stat_lane >= HEAD)), 1.0, 0.0
    ).astype(BF16)

    def attend(first):
        query = qbuf[pl.ds(first, 2)].reshape(ROWS, HEAD).astype(F32) * score_scale
        high = query.astype(BF16)
        low = (query - high.astype(F32)).astype(BF16)
        both = jnp.concatenate([high, low], axis=1)
        best = None
        for c in range(chunks):
            kt = ktbuf[:, keys_of(c)]
            scores = jnp.dot(both, jnp.concatenate([kt, kt], axis=0), preferred_element_type=F32)
            sbuf[:, keys_of(c)] = scores
            for part in range(KEY_CHUNK // 128):
                piece = scores[:, part * 128 : (part + 1) * 128]
                best = piece if best is None else jnp.maximum(best, piece)
        row_max = jnp.max(best, axis=1, keepdims=True)
        total = jnp.zeros((ROWS, 2 * HEAD), F32)
        for c in range(chunks):
            weights = jnp.exp2(sbuf[:, keys_of(c)] - row_max).astype(BF16)
            slots = slice(c * KEY_CHUNK // TOK, (c + 1) * KEY_CHUNK // TOK)
            values = kvbuf[slots, 1].reshape(KEY_CHUNK, HEAD)
            total += jnp.dot(weights, jnp.concatenate([values, ones], axis=1), preferred_element_type=F32)
        attended = (total[:, :HEAD] * (value_scale / total[:, HEAD:])).astype(BF16)
        pairs = [
            jnp.concatenate([attended[k * TOK : k * TOK + LAT], attended[k * TOK + LAT : (k + 1) * TOK]], axis=1)
            for k in range(2)
        ]
        partial = jnp.dot(jnp.concatenate(pairs, axis=0), wblk[...], preferred_element_type=F32)
        partial = partial[:, :128] + partial[:, 128:]
        as_float = attended.astype(F32)
        square = as_float * as_float
        square_high = square.astype(BF16)
        square_low = (square - square_high.astype(F32)).astype(BF16)
        stats = lax.dot_general(
            picker,
            jnp.concatenate([attended, square_high, square_low], axis=1),
            (((1,), (1,)), ((), ())),
            preferred_element_type=F32,
        )[0:8]
        for k in range(2):
            pbuf[first + k, 0:LAT] = partial[k * LAT : (k + 1) * LAT]
            pbuf[first + k, LAT:PACK] = stats[:, k * TOK : (k + 1) * TOK] + consts[...]

    def one_group(g, _):
        with jax.named_scope("attend"):
            for half in range(2):
                for k in range(2):
                    j = g * NY + half * 2 + k

                    @pl.when(j < SEQ - 1)
                    def _():
                        q_copy(j).wait_recv()

                    @pl.when(j == SEQ - 1)
                    def _():
                        own_query.wait()

                attend(g * NY + half * 2)
            for i in range(NY - 1):
                y_copy(g, i).start()

        @pl.when(g > 0)
        def _():
            with jax.named_scope("join"):
                join_y(g - 1)
                z_copy(g - 1).start()

        return 0

    lax.fori_loop(0, NZ, one_group, 0)

    with jax.named_scope("tail"):
        join_y(NZ - 1)
        total = zsend[NZ - 1]
        for g in range(NZ - 1):
            z_copy(g).wait_recv()
            total = total + zbuf[g]

        center = total[LAT : LAT + 1] * (1.0 / WIDTH)
        spread = jnp.maximum(total[LAT + 1 : LAT + 2] * (1.0 / WIDTH) - center * center, 0.0)
        inverse = lax.rsqrt(spread + 1e-06)
        rows = lax.broadcasted_iota(jnp.int32, (128, 128), 0)
        stacked = jnp.where(rows == 0, inverse, jnp.where(rows == 1, center * inverse, 0.0)).T
        left = lax.broadcasted_iota(jnp.int32, (LAT, 128), 1) < LAT
        inverse_at = jnp.where(left, stacked[0:LAT, 0:1], stacked[LAT:, 0:1])
        center_at = jnp.where(left, stacked[0:LAT, 1:2], stacked[LAT:, 1:2])
        velocity = (
            inverse_at * total[0:LAT]
            - center_at * total[LAT + 2 : LAT + 3]
            + total[LAT + 3 : LAT + 4]
        )

        @pl.when(tm < TM - 1)
        def _():
            time_copy.wait_recv()

        @pl.when(tm == TM - 1)
        def _():
            later[1] = jnp.zeros((8, 128), F32)

        step = (later[1] - time_now) / 1000.0
        drift = velocity * step[0:1]
        tsend[...] = drift

        def t_copy(k):
            return pltpu.make_async_remote_copy(
                src_ref=tsend,
                dst_ref=tbuf.at[k - 1],
                send_sem=t_send.at[k - 1],
                recv_sem=t_recv.at[k - 1],
                device_id=((tm + k) % TM, me),
                device_id_type=MESH,
            )

        for k in range(1, TM):

            @pl.when(tm + k < TM)
            def _():
                t_copy(k).start()

        lat[0:LAT] = drift

        for k in range(1, TM):

            @pl.when(tm >= k)
            def _():
                t_copy(k).wait_recv()
                lat[0:LAT] += tbuf[k - 1]

        summed = lat[0:LAT]
        lat[LAT : 2 * LAT] = pltpu.roll(summed, LAT, 1)
        even = lat[pl.ds(0, LAT, stride=2)]
        odd = lat[pl.ds(1, LAT, stride=2)]
        out[...] = start_latent[...] + jnp.where(left, even, pltpu.roll(odd, LAT, 1))

    with jax.named_scope("drain"):

        def drain(j, _):
            kv_copy(j).wait_send()
            q_copy(j).wait_send()
            return 0

        lax.fori_loop(0, SEQ - 1, drain, 0)

        def drain_group(g, _):
            for i in range(NY - 1):
                y_copy(g, i).wait_send()

            @pl.when(g < NZ - 1)
            def _():
                z_copy(g).wait_send()

            return 0

        lax.fori_loop(0, NZ, drain_group, 0)
        for k in range(1, TM):

            @pl.when(tm + k < TM)
            def _():
                t_copy(k).wait_send()

        @pl.when(tm > 0)
        def _():
            time_copy.wait_send()


def body(projected, scale_table, group_index, timesteps, time_weight, head_weight, start_latent):
    codes = projected[0].transpose(1, 0, 2)
    table = scale_table.transpose(1, 0, 2)
    half = FREQ // 2
    values = np.power(np.float64(10000.0), -np.arange(half, dtype=np.float64) / half).astype(np.float32)
    freqs = jnp.asarray(np.repeat(np.concatenate([values, values]), 2)[None, :])
    any_space = pl.BlockSpec(memory_space=pl.ANY)
    vmem = pl.BlockSpec(memory_space=pltpu.VMEM)
    smem = pl.BlockSpec(memory_space=pltpu.SMEM)
    dma = pltpu.SemaphoreType.DMA
    latents = pl.pallas_call(
        kernel,
        name="window",
        out_shape=jax.ShapeDtypeStruct((LAT, 128), F32),
        in_specs=[any_space, vmem, smem, smem, vmem, any_space, any_space, vmem],
        out_specs=vmem,
        scratch_shapes=[
            pltpu.VMEM((SEQ, TOK, HEAD), BF16),
            pltpu.VMEM((SEQ, 2, TOK, HEAD), BF16),
            pltpu.VMEM((HEAD, KEYS), BF16),
            pltpu.VMEM((ROWS, KEYS), F32),
            pltpu.VMEM((2 * HEAD, 256), BF16),
            pltpu.VMEM((FREQ, 2, HEAD), BF16),
            pltpu.VMEM((LAT, HEAD), BF16),
            pltpu.VMEM((8, 128), F32),
            pltpu.VMEM((SEQ, PACK, 128), F32),
            pltpu.VMEM((SEQ, PACK, 128), F32),
            pltpu.VMEM((NZ, PACK, 128), F32),
            pltpu.VMEM((NZ, PACK, 128), F32),
            pltpu.VMEM((LAT, 128), F32),
            pltpu.VMEM((TM - 1, LAT, 128), F32),
            pltpu.VMEM((2, 8, 128), F32),
            pltpu.VMEM((2 * LAT, 128), F32),
            dma((SEQ,)),
            dma((SEQ,)),
            dma((SEQ,)),
            dma((SEQ,)),
            dma((SEQ,)),
            dma((SEQ,)),
            dma((NZ,)),
            dma((NZ,)),
            dma((TM - 1,)),
            dma((TM - 1,)),
            dma((6,)),
        ],
        compiler_params=pltpu.CompilerParams(
            collective_id=0, has_side_effects=True, vmem_limit_bytes=40 << 20
        ),
    )(codes, table, group_index, timesteps, freqs, time_weight, head_weight, start_latent)
    return latents[None]


def solution(mesh):
    placed = (P("tm", "seq", None, None), P(), P("tm"), P("tm"), P(), P(), P("seq", None))
    return jax.shard_map(
        body, mesh=mesh, in_specs=placed, out_specs=P("tm", "seq", None), check_vma=False
    )
```

```python
import functools
import math

import jax
import jax.numpy as jnp
import numpy as np
from jax import lax
from jax.experimental import pallas as pl
from jax.experimental.pallas import tpu as pltpu
from jax.sharding import PartitionSpec as P

MESH = pl.DeviceIdType.MESH
F32 = jnp.float32
BF16 = jnp.bfloat16

NY, NZ, TM = 4, 8, 8
SEQ = NY * NZ
TOK = 128
HEAD = 128
LAT = 64
KEYS = SEQ * TOK
WIDTH = SEQ * HEAD
FREQ = 256
ROWS = 256
KEY_CHUNK = 512
PACK = 72


def group_dz(g):
    odd = g % 2
    return (odd * ((g + 1) // 2) - (1 - odd) * (g // 2)) % NZ


def group_dy(i):
    return (i + 1) % NY


OWN = NY - 1
OTHERS = [j for j in range(SEQ) if j != OWN]


def kernel(
    proj,
    table_hbm,
    group_index,
    timesteps,
    freqs_hbm,
    time_weight,
    head_weight,
    latent_hbm,
    out,
    qbuf,
    kvbuf,
    ktbuf,
    sbuf,
    wblk,
    tw,
    hw,
    consts,
    scale_table,
    freqs,
    start_latent,
    mbuf,
    pbuf,
    ybuf,
    zsend,
    zbuf,
    tsend,
    tbuf,
    later,
    lat,
    kv_send,
    kv_recv,
    q_send,
    q_recv,
    y_send,
    y_recv,
    z_send,
    z_recv,
    t_send,
    t_recv,
    misc,
):
    tm = lax.axis_index("tm")
    me = lax.axis_index("seq")
    my, mz = me // NZ, me % NZ

    def seq_at(dy, dz):
        return ((my + dy + NY) % NY) * NZ + (mz + dz + NZ) % NZ

    def peer(dy, dz):
        return (tm, seq_at(dy, dz))

    cols = pl.ds(pl.multiple_of(me * HEAD, HEAD), HEAD)
    own_codes = pltpu.make_async_copy(proj.at[1:3, :, cols], kvbuf.at[OWN], misc.at[0])
    own_query = pltpu.make_async_copy(proj.at[0, :, cols], qbuf.at[OWN], misc.at[1])
    get_table = pltpu.make_async_copy(table_hbm, scale_table, misc.at[6])
    get_freqs = pltpu.make_async_copy(freqs_hbm, freqs, misc.at[7])
    get_latent = pltpu.make_async_copy(latent_hbm, start_latent, misc.at[8])
    get_table.start()
    get_freqs.start()
    get_latent.start()
    get_tw = pltpu.make_async_copy(time_weight.at[:, :, cols], tw, misc.at[2])
    get_hw = pltpu.make_async_copy(head_weight.at[:, cols], hw, misc.at[3])
    own_codes.start()
    own_query.start()
    get_tw.start()
    get_hw.start()

    barrier = pltpu.get_barrier_semaphore()

    def greet(o, _):
        pl.semaphore_signal(barrier, inc=1, device_id=(tm, (me + o) % SEQ), device_id_type=MESH)
        return 0

    def greet_tm(o, _):
        pl.semaphore_signal(barrier, inc=1, device_id=((tm + o) % TM, me), device_id_type=MESH)
        return 0

    with jax.named_scope("barrier"):
        lax.fori_loop(1, SEQ, greet, 0)
        lax.fori_loop(1, TM, greet_tm, 0)
        pl.semaphore_wait(barrier, SEQ + TM - 2)

    def kv_copy(j):
        g, i = j // NY, j % NY
        to = seq_at(-group_dy(i), -group_dz(g))
        lanes = pl.ds(pl.multiple_of(to * HEAD, HEAD), HEAD)
        return pltpu.make_async_remote_copy(
            src_ref=proj.at[1:3, :, lanes],
            dst_ref=kvbuf.at[j],
            send_sem=kv_send.at[j],
            recv_sem=kv_recv.at[j],
            device_id=(tm, to),
            device_id_type=MESH,
        )

    def q_copy(j):
        g, i = j // NY, j % NY
        to = seq_at(-group_dy(i), -group_dz(g))
        lanes = pl.ds(pl.multiple_of(to * HEAD, HEAD), HEAD)
        return pltpu.make_async_remote_copy(
            src_ref=proj.at[0, :, lanes],
            dst_ref=qbuf.at[j],
            send_sem=q_send.at[j],
            recv_sem=q_recv.at[j],
            device_id=(tm, to),
            device_id_type=MESH,
        )

    with jax.named_scope("send"):
        for j in OTHERS:
            kv_copy(j).start()
        for j in OTHERS:
            q_copy(j).start()

    time_copy = pltpu.make_async_remote_copy(
        src_ref=later.at[0],
        dst_ref=later.at[1],
        send_sem=misc.at[4],
        recv_sem=misc.at[5],
        device_id=((tm + TM - 1) % TM, me),
        device_id_type=MESH,
    )
    time_now = jnp.full((8, 128), timesteps[0], jnp.int32).astype(F32)
    later[0] = time_now

    @pl.when(tm > 0)
    def _():
        time_copy.start()

    with jax.named_scope("constants"):
        get_table.wait()
        get_freqs.wait()
        get_latent.wait()
        row = lax.broadcasted_iota(jnp.int32, (8, 128), 0)
        head_lane = lax.broadcasted_iota(jnp.int32, (8, SEQ), 1)
        group_row = lax.broadcasted_iota(jnp.int32, (8, SEQ), 0)
        chosen = (head_lane == me) & (group_row == group_index[0])

        def pick(k):
            kept = jnp.where(chosen, scale_table[k], 0.0)
            return jnp.sum(jnp.sum(kept, axis=1, keepdims=True), axis=0, keepdims=True)

        factor = pick(0) * pick(1) / math.sqrt(HEAD)
        score_scale = factor * math.log2(math.e)
        value_scale = pick(2)

        angles = time_now[0:1, 0:1] * freqs[...]
        wide_lane = lax.broadcasted_iota(jnp.int32, (8, 2 * FREQ), 1)
        wide_row = lax.broadcasted_iota(jnp.int32, (8, 2 * FREQ), 0)
        waves = jnp.where(wide_lane < FREQ, jnp.cos(angles), jnp.sin(angles))
        waves = jnp.where(wide_lane % 2 == wide_row, waves, 0.0).astype(BF16)
        get_tw.wait()
        get_hw.wait()
        modulation = jnp.dot(waves, tw[...].reshape(2 * FREQ, HEAD), preferred_element_type=F32)
        shift, scale = modulation[0:1], modulation[1:2]
        weight = hw[...].astype(F32)
        weight = jnp.concatenate([weight, weight], axis=0)
        scaled = (weight * (1.0 + scale)).T
        shifted = jnp.sum((weight * shift).T, axis=0, keepdims=True)
        high = scaled.astype(BF16)
        low = (scaled - high.astype(F32)).astype(BF16)
        left = lax.broadcasted_iota(jnp.int32, (HEAD, 128), 1) < LAT
        zero = jnp.zeros_like(high)
        wblk[0:HEAD, 0:128] = jnp.where(left, high, zero)
        wblk[0:HEAD, 128:256] = jnp.where(left, low, zero)
        wblk[HEAD : 2 * HEAD, 0:128] = jnp.where(left, zero, high)
        wblk[HEAD : 2 * HEAD, 128:256] = jnp.where(left, zero, low)
        summed = jnp.sum(high.astype(F32) + low.astype(F32), axis=0, keepdims=True)
        consts[...] = jnp.where(row == 2, summed, jnp.where(row == 3, shifted, 0.0))

    with jax.named_scope("keys"):
        for j in range(SEQ):
            if j == OWN:
                own_codes.wait()
            else:
                kv_copy(j).wait_recv()
            ktbuf[:, j * TOK : (j + 1) * TOK] = kvbuf[j, 0].T

    def y_copy(g, i):
        return pltpu.make_async_remote_copy(
            src_ref=pbuf.at[g * NY + i],
            dst_ref=ybuf.at[g * NY + i],
            send_sem=y_send.at[g * NY + i],
            recv_sem=y_recv.at[g * NY + i],
            device_id=peer(group_dy(i), 0),
            device_id_type=MESH,
        )

    def z_copy(g):
        return pltpu.make_async_remote_copy(
            src_ref=zsend.at[g],
            dst_ref=zbuf.at[g],
            send_sem=z_send.at[g],
            recv_sem=z_recv.at[g],
            device_id=peer(0, group_dz(g)),
            device_id_type=MESH,
        )

    def join_y(g):
        total = pbuf[g * NY + NY - 1]
        for i in range(NY - 1):
            y_copy(g, i).wait_recv()
            total = total + ybuf[g * NY + i]
        zsend[g] = total

    keys_of = lambda c: slice(c * KEY_CHUNK, (c + 1) * KEY_CHUNK)
    chunks = KEYS // KEY_CHUNK
    ones = jnp.ones((KEY_CHUNK, 128), BF16)
    stat_row = lax.broadcasted_iota(jnp.int32, (16, 3 * HEAD), 0)
    stat_lane = lax.broadcasted_iota(jnp.int32, (16, 3 * HEAD), 1)
    picker = jnp.where(
        ((stat_row == 0) & (stat_lane < HEAD)) | ((stat_row == 1) & (stat_lane >= HEAD)), 1.0, 0.0
    ).astype(BF16)

    def load_query(n):
        query = qbuf[pl.ds(2 * n, 2)].reshape(ROWS, HEAD).astype(F32) * score_scale
        high = query.astype(BF16)
        low = (query - high.astype(F32)).astype(BF16)
        return jnp.concatenate([high, low], axis=1)

    def score(both, c, slot, best):
        kt = ktbuf[:, keys_of(c)]
        scores = jnp.dot(both, jnp.concatenate([kt, kt], axis=0), preferred_element_type=F32)
        sbuf[slot, :, keys_of(c)] = scores
        for part in range(KEY_CHUNK // 128):
            piece = scores[:, part * 128 : (part + 1) * 128]
            best = piece if best is None else jnp.maximum(best, piece)
        return best

    def keep_max(slot, best):
        mbuf[slot] = jnp.broadcast_to(jnp.max(best, axis=1, keepdims=True), (ROWS, 128))

    def blend(slot, c, row_max):
        weights = jnp.exp2(sbuf[slot, :, keys_of(c)] - row_max).astype(BF16)
        slots = slice(c * KEY_CHUNK // TOK, (c + 1) * KEY_CHUNK // TOK)
        values = kvbuf[slots, 1].reshape(KEY_CHUNK, HEAD)
        return jnp.dot(weights, jnp.concatenate([values, ones], axis=1), preferred_element_type=F32)

    def finish(first, total):
        attended = (total[:, :HEAD] * (value_scale / total[:, HEAD:])).astype(BF16)
        pairs = [
            jnp.concatenate([attended[k * TOK : k * TOK + LAT], attended[k * TOK + LAT : (k + 1) * TOK]], axis=1)
            for k in range(2)
        ]
        partial = jnp.dot(jnp.concatenate(pairs, axis=0), wblk[...], preferred_element_type=F32)
        partial = partial[:, :128] + partial[:, 128:]
        as_float = attended.astype(F32)
        square = as_float * as_float
        square_high = square.astype(BF16)
        square_low = (square - square_high.astype(F32)).astype(BF16)
        stats = lax.dot_general(
            picker,
            jnp.concatenate([attended, square_high, square_low], axis=1),
            (((1,), (1,)), ((), ())),
            preferred_element_type=F32,
        )[0:8]
        for k in range(2):
            pbuf[first + k, 0:LAT] = partial[k * LAT : (k + 1) * LAT]
            pbuf[first + k, LAT:PACK] = stats[:, k * TOK : (k + 1) * TOK] + consts[...]

    def block(n, slot):
        both = load_query(jnp.minimum(n + 1, SEQ // 2 - 1))
        row_max = mbuf[slot][:, 0:1]
        best = None
        total = jnp.zeros((ROWS, 2 * HEAD), F32)
        for c in range(chunks):
            best = score(both, c, 1 - slot, best)
            total += blend(slot, c, row_max)
        keep_max(1 - slot, best)
        finish(2 * n, total)

    with jax.named_scope("first"):
        q_copy(0).wait_recv()
        q_copy(1).wait_recv()
        both = load_query(0)
        best = None
        for c in range(chunks):
            best = score(both, c, 0, best)
        keep_max(0, best)

    def one_group(g, _):
        with jax.named_scope("attend"):
            q_copy(g * NY + 2).wait_recv()

            @pl.when(g > 0)
            def _():
                q_copy(g * NY + 3).wait_recv()

            @pl.when(g == 0)
            def _():
                own_query.wait()

            block(2 * g, 0)
            y_copy(g, 0).start()
            y_copy(g, 1).start()

        with jax.named_scope("attend"):

            @pl.when(g < NZ - 1)
            def _():
                q_copy(g * NY + 4).wait_recv()
                q_copy(g * NY + 5).wait_recv()

            block(2 * g + 1, 1)
            y_copy(g, 2).start()

        @pl.when(g > 0)
        def _():
            with jax.named_scope("join"):
                join_y(g - 1)

                @pl.when(g > 1)
                def _():
                    z_copy(g - 1).start()

        return 0

    lax.fori_loop(0, NZ, one_group, 0)

    with jax.named_scope("tail"):
        join_y(NZ - 1)
        z_copy(NZ - 1).start()
        total = zsend[0]
        for g in range(1, NZ):
            z_copy(g).wait_recv()
            total = total + zbuf[g]

        center = total[LAT : LAT + 1] * (1.0 / WIDTH)
        spread = jnp.maximum(total[LAT + 1 : LAT + 2] * (1.0 / WIDTH) - center * center, 0.0)
        inverse = lax.rsqrt(spread + 1e-06)
        rows = lax.broadcasted_iota(jnp.int32, (128, 128), 0)
        stacked = jnp.where(rows == 0, inverse, jnp.where(rows == 1, center * inverse, 0.0)).T
        left = lax.broadcasted_iota(jnp.int32, (LAT, 128), 1) < LAT
        inverse_at = jnp.where(left, stacked[0:LAT, 0:1], stacked[LAT:, 0:1])
        center_at = jnp.where(left, stacked[0:LAT, 1:2], stacked[LAT:, 1:2])
        velocity = (
            inverse_at * total[0:LAT]
            - center_at * total[LAT + 2 : LAT + 3]
            + total[LAT + 3 : LAT + 4]
        )

        @pl.when(tm < TM - 1)
        def _():
            time_copy.wait_recv()

        @pl.when(tm == TM - 1)
        def _():
            later[1] = jnp.zeros((8, 128), F32)

        step = (later[1] - time_now) / 1000.0
        drift = velocity * step[0:1]
        tsend[...] = drift

        def t_copy(k):
            return pltpu.make_async_remote_copy(
                src_ref=tsend,
                dst_ref=tbuf.at[k - 1],
                send_sem=t_send.at[k - 1],
                recv_sem=t_recv.at[k - 1],
                device_id=((tm + k) % TM, me),
                device_id_type=MESH,
            )

        for k in range(1, TM):

            @pl.when(tm + k < TM)
            def _():
                t_copy(k).start()

        lat[0:LAT] = drift

        for k in range(1, TM):

            @pl.when(tm >= k)
            def _():
                t_copy(k).wait_recv()
                lat[0:LAT] += tbuf[k - 1]

        summed = lat[0:LAT]
        lat[LAT : 2 * LAT] = pltpu.roll(summed, LAT, 1)
        even = lat[pl.ds(0, LAT, stride=2)]
        odd = lat[pl.ds(1, LAT, stride=2)]
        out[...] = start_latent[...] + jnp.where(left, even, pltpu.roll(odd, LAT, 1))

    with jax.named_scope("drain"):

        for j in OTHERS:
            kv_copy(j).wait_send()
            q_copy(j).wait_send()

        def drain_group(g, _):
            for i in range(NY - 1):
                y_copy(g, i).wait_send()

            @pl.when(g > 0)
            def _():
                z_copy(g).wait_send()

            return 0

        lax.fori_loop(0, NZ, drain_group, 0)
        for k in range(1, TM):

            @pl.when(tm + k < TM)
            def _():
                t_copy(k).wait_send()

        @pl.when(tm > 0)
        def _():
            time_copy.wait_send()


def body(projected, scale_table, group_index, timesteps, time_weight, head_weight, start_latent):
    codes = projected[0].transpose(1, 0, 2)
    table = scale_table.transpose(1, 0, 2)
    half = FREQ // 2
    values = np.power(np.float64(10000.0), -np.arange(half, dtype=np.float64) / half).astype(np.float32)
    freqs = jnp.asarray(np.repeat(np.concatenate([values, values]), 2)[None, :])
    any_space = pl.BlockSpec(memory_space=pl.ANY)
    vmem = pl.BlockSpec(memory_space=pltpu.VMEM)
    smem = pl.BlockSpec(memory_space=pltpu.SMEM)
    dma = pltpu.SemaphoreType.DMA
    latents = pl.pallas_call(
        kernel,
        name="window",
        out_shape=jax.ShapeDtypeStruct((LAT, 128), F32),
        in_specs=[any_space, any_space, smem, smem, any_space, any_space, any_space, any_space],
        out_specs=vmem,
        scratch_shapes=[
            pltpu.VMEM((SEQ, TOK, HEAD), BF16),
            pltpu.VMEM((SEQ, 2, TOK, HEAD), BF16),
            pltpu.VMEM((HEAD, KEYS), BF16),
            pltpu.VMEM((2, ROWS, KEYS), F32),
            pltpu.VMEM((2 * HEAD, 256), BF16),
            pltpu.VMEM((FREQ, 2, HEAD), BF16),
            pltpu.VMEM((LAT, HEAD), BF16),
            pltpu.VMEM((8, 128), F32),
            pltpu.VMEM((3, 8, SEQ), F32),
            pltpu.VMEM((1, 2 * FREQ), F32),
            pltpu.VMEM((LAT, 128), F32),
            pltpu.VMEM((2, ROWS, 128), F32),
            pltpu.VMEM((SEQ, PACK, 128), F32),
            pltpu.VMEM((SEQ, PACK, 128), F32),
            pltpu.VMEM((NZ, PACK, 128), F32),
            pltpu.VMEM((NZ, PACK, 128), F32),
            pltpu.VMEM((LAT, 128), F32),
            pltpu.VMEM((TM - 1, LAT, 128), F32),
            pltpu.VMEM((2, 8, 128), F32),
            pltpu.VMEM((2 * LAT, 128), F32),
            dma((SEQ,)),
            dma((SEQ,)),
            dma((SEQ,)),
            dma((SEQ,)),
            dma((SEQ,)),
            dma((SEQ,)),
            dma((NZ,)),
            dma((NZ,)),
            dma((TM - 1,)),
            dma((TM - 1,)),
            dma((9,)),
        ],
        compiler_params=pltpu.CompilerParams(
            collective_id=0, has_side_effects=True, vmem_limit_bytes=60 << 20
        ),
    )(codes, table, group_index, timesteps, freqs, time_weight, head_weight, start_latent)
    return latents[None]


def solution(mesh):
    placed = (P("tm", "seq", None, None), P(), P("tm"), P("tm"), P(), P(), P("seq", None))
    return jax.shard_map(
        body, mesh=mesh, in_specs=placed, out_specs=P("tm", "seq", None), check_vma=False
    )
```

```python
import functools
import math

import jax
import jax.numpy as jnp
import numpy as np
from jax import lax
from jax.experimental import pallas as pl
from jax.experimental.pallas import tpu as pltpu
from jax.sharding import PartitionSpec as P

MESH = pl.DeviceIdType.MESH
F32 = jnp.float32
BF16 = jnp.bfloat16

NY, NZ, TM = 4, 8, 8
SEQ = NY * NZ
TOK = 128
HEAD = 128
LAT = 64
KEYS = SEQ * TOK
WIDTH = SEQ * HEAD
FREQ = 256
ROWS = 256
KEY_CHUNK = 512
PACK = 72


def group_dz(g):
    odd = g % 2
    return (odd * ((g + 1) // 2) - (1 - odd) * (g // 2)) % NZ


def group_dy(i):
    return (i + 1) % NY


OWN = NY - 1
OTHERS = [j for j in range(SEQ) if j != OWN]


def kernel(
    proj,
    table_hbm,
    group_index,
    timesteps,
    freqs_hbm,
    time_weight,
    head_weight,
    latent_hbm,
    out,
    qbuf,
    kvbuf,
    ktbuf,
    sbuf,
    wblk,
    tw,
    hw,
    consts,
    scale_table,
    freqs,
    start_latent,
    mbuf,
    acc,
    pbuf,
    ybuf,
    zsend,
    zbuf,
    tsend,
    tbuf,
    later,
    lat,
    kv_send,
    kv_recv,
    q_send,
    q_recv,
    y_send,
    y_recv,
    z_send,
    z_recv,
    t_send,
    t_recv,
    misc,
):
    tm = lax.axis_index("tm")
    me = lax.axis_index("seq")
    my, mz = me // NZ, me % NZ

    def seq_at(dy, dz):
        return ((my + dy + NY) % NY) * NZ + (mz + dz + NZ) % NZ

    def peer(dy, dz):
        return (tm, seq_at(dy, dz))

    cols = pl.ds(pl.multiple_of(me * HEAD, HEAD), HEAD)
    own_codes = pltpu.make_async_copy(proj.at[1:3, :, cols], kvbuf.at[OWN], misc.at[0])
    own_query = pltpu.make_async_copy(proj.at[0, :, cols], qbuf.at[OWN], misc.at[1])
    get_table = pltpu.make_async_copy(table_hbm, scale_table, misc.at[6])
    get_freqs = pltpu.make_async_copy(freqs_hbm, freqs, misc.at[7])
    get_latent = pltpu.make_async_copy(latent_hbm, start_latent, misc.at[8])
    get_table.start()
    get_freqs.start()
    get_latent.start()
    get_tw = pltpu.make_async_copy(time_weight.at[:, :, cols], tw, misc.at[2])
    get_hw = pltpu.make_async_copy(head_weight.at[:, cols], hw, misc.at[3])
    own_codes.start()
    own_query.start()
    get_tw.start()
    get_hw.start()

    barrier = pltpu.get_barrier_semaphore()

    def greet(o, _):
        pl.semaphore_signal(barrier, inc=1, device_id=(tm, (me + o) % SEQ), device_id_type=MESH)
        return 0

    def greet_tm(o, _):
        pl.semaphore_signal(barrier, inc=1, device_id=((tm + o) % TM, me), device_id_type=MESH)
        return 0

    with jax.named_scope("barrier"):
        lax.fori_loop(1, SEQ, greet, 0)
        lax.fori_loop(1, TM, greet_tm, 0)
        pl.semaphore_wait(barrier, SEQ + TM - 2)

    def kv_copy(j):
        g, i = j // NY, j % NY
        to = seq_at(-group_dy(i), -group_dz(g))
        lanes = pl.ds(pl.multiple_of(to * HEAD, HEAD), HEAD)
        return pltpu.make_async_remote_copy(
            src_ref=proj.at[1:3, :, lanes],
            dst_ref=kvbuf.at[j],
            send_sem=kv_send.at[j],
            recv_sem=kv_recv.at[j],
            device_id=(tm, to),
            device_id_type=MESH,
        )

    def q_copy(j):
        g, i = j // NY, j % NY
        to = seq_at(-group_dy(i), -group_dz(g))
        lanes = pl.ds(pl.multiple_of(to * HEAD, HEAD), HEAD)
        return pltpu.make_async_remote_copy(
            src_ref=proj.at[0, :, lanes],
            dst_ref=qbuf.at[j],
            send_sem=q_send.at[j],
            recv_sem=q_recv.at[j],
            device_id=(tm, to),
            device_id_type=MESH,
        )

    with jax.named_scope("send"):
        for j in OTHERS:
            if j < NY:
                q_copy(j).start()
        for j in OTHERS:
            kv_copy(j).start()
        for j in OTHERS:
            if j >= NY:
                q_copy(j).start()

    time_copy = pltpu.make_async_remote_copy(
        src_ref=later.at[0],
        dst_ref=later.at[1],
        send_sem=misc.at[4],
        recv_sem=misc.at[5],
        device_id=((tm + TM - 1) % TM, me),
        device_id_type=MESH,
    )
    time_now = jnp.full((8, 128), timesteps[0], jnp.int32).astype(F32)
    later[0] = time_now

    @pl.when(tm > 0)
    def _():
        time_copy.start()

    with jax.named_scope("constants"):
        get_table.wait()
        get_freqs.wait()
        get_latent.wait()
        row = lax.broadcasted_iota(jnp.int32, (8, 128), 0)
        head_lane = lax.broadcasted_iota(jnp.int32, (8, SEQ), 1)
        group_row = lax.broadcasted_iota(jnp.int32, (8, SEQ), 0)
        chosen = (head_lane == me) & (group_row == group_index[0])

        def pick(k):
            kept = jnp.where(chosen, scale_table[k], 0.0)
            return jnp.sum(jnp.sum(kept, axis=1, keepdims=True), axis=0, keepdims=True)

        factor = pick(0) * pick(1) / math.sqrt(HEAD)
        score_scale = factor * math.log2(math.e)
        value_scale = pick(2)

        angles = time_now[0:1, 0:1] * freqs[...]
        wide_lane = lax.broadcasted_iota(jnp.int32, (8, 2 * FREQ), 1)
        wide_row = lax.broadcasted_iota(jnp.int32, (8, 2 * FREQ), 0)
        waves = jnp.where(wide_lane < FREQ, jnp.cos(angles), jnp.sin(angles))
        waves = jnp.where(wide_lane % 2 == wide_row, waves, 0.0).astype(BF16)
        get_tw.wait()
        get_hw.wait()
        modulation = jnp.dot(waves, tw[...].reshape(2 * FREQ, HEAD), preferred_element_type=F32)
        shift, scale = modulation[0:1], modulation[1:2]
        weight = hw[...].astype(F32)
        weight = jnp.concatenate([weight, weight], axis=0)
        scaled = (weight * (1.0 + scale)).T
        shifted = jnp.sum((weight * shift).T, axis=0, keepdims=True)
        high = scaled.astype(BF16)
        low = (scaled - high.astype(F32)).astype(BF16)
        left = lax.broadcasted_iota(jnp.int32, (HEAD, 128), 1) < LAT
        zero = jnp.zeros_like(high)
        wblk[0:HEAD, 0:128] = jnp.where(left, high, zero)
        wblk[0:HEAD, 128:256] = jnp.where(left, low, zero)
        wblk[HEAD : 2 * HEAD, 0:128] = jnp.where(left, zero, high)
        wblk[HEAD : 2 * HEAD, 128:256] = jnp.where(left, zero, low)
        summed = jnp.sum(high.astype(F32) + low.astype(F32), axis=0, keepdims=True)
        consts[...] = jnp.where(row == 2, summed, jnp.where(row == 3, shifted, 0.0))


    def y_copy(g, i):
        return pltpu.make_async_remote_copy(
            src_ref=pbuf.at[g * NY + i],
            dst_ref=ybuf.at[g * NY + i],
            send_sem=y_send.at[g * NY + i],
            recv_sem=y_recv.at[g * NY + i],
            device_id=peer(group_dy(i), 0),
            device_id_type=MESH,
        )

    def z_copy(g):
        return pltpu.make_async_remote_copy(
            src_ref=zsend.at[g],
            dst_ref=zbuf.at[g],
            send_sem=z_send.at[g],
            recv_sem=z_recv.at[g],
            device_id=peer(0, group_dz(g)),
            device_id_type=MESH,
        )

    def join_y(g):
        total = pbuf[g * NY + NY - 1]
        for i in range(NY - 1):
            y_copy(g, i).wait_recv()
            total = total + ybuf[g * NY + i]
        zsend[g] = total

    keys_of = lambda c: slice(c * KEY_CHUNK, (c + 1) * KEY_CHUNK)
    chunks = KEYS // KEY_CHUNK
    ones = jnp.ones((KEY_CHUNK, 128), BF16)
    stat_row = lax.broadcasted_iota(jnp.int32, (16, 3 * HEAD), 0)
    stat_lane = lax.broadcasted_iota(jnp.int32, (16, 3 * HEAD), 1)
    picker = jnp.where(
        ((stat_row == 0) & (stat_lane < HEAD)) | ((stat_row == 1) & (stat_lane >= HEAD)), 1.0, 0.0
    ).astype(BF16)

    def load_query(n):
        query = qbuf[pl.ds(2 * n, 2)].reshape(ROWS, HEAD).astype(F32) * score_scale
        high = query.astype(BF16)
        low = (query - high.astype(F32)).astype(BF16)
        return jnp.concatenate([high, low], axis=1)

    def score(both, c, slot, best):
        kt = ktbuf[:, keys_of(c)]
        scores = jnp.dot(both, jnp.concatenate([kt, kt], axis=0), preferred_element_type=F32)
        sbuf[slot, :, keys_of(c)] = scores
        for part in range(KEY_CHUNK // 128):
            piece = scores[:, part * 128 : (part + 1) * 128]
            best = piece if best is None else jnp.maximum(best, piece)
        return best

    def keep_max(slot, best):
        mbuf[slot] = jnp.broadcast_to(jnp.max(best, axis=1, keepdims=True), (ROWS, 128))

    def blend(slot, c, row_max):
        weights = jnp.exp2(sbuf[slot, :, keys_of(c)] - row_max).astype(BF16)
        slots = slice(c * KEY_CHUNK // TOK, (c + 1) * KEY_CHUNK // TOK)
        values = kvbuf[slots, 1].reshape(KEY_CHUNK, HEAD)
        return jnp.dot(weights, jnp.concatenate([values, ones], axis=1), preferred_element_type=F32)

    def finish(first, total):
        attended = (total[:, :HEAD] * (value_scale / total[:, HEAD:])).astype(BF16)
        pairs = [
            jnp.concatenate([attended[k * TOK : k * TOK + LAT], attended[k * TOK + LAT : (k + 1) * TOK]], axis=1)
            for k in range(2)
        ]
        partial = jnp.dot(jnp.concatenate(pairs, axis=0), wblk[...], preferred_element_type=F32)
        partial = partial[:, :128] + partial[:, 128:]
        as_float = attended.astype(F32)
        square = as_float * as_float
        square_high = square.astype(BF16)
        square_low = (square - square_high.astype(F32)).astype(BF16)
        stats = lax.dot_general(
            picker,
            jnp.concatenate([attended, square_high, square_low], axis=1),
            (((1,), (1,)), ((), ())),
            preferred_element_type=F32,
        )[0:8]
        for k in range(2):
            pbuf[first + k, 0:LAT] = partial[k * LAT : (k + 1) * LAT]
            pbuf[first + k, LAT:PACK] = stats[:, k * TOK : (k + 1) * TOK] + consts[...]

    def block(n, slot, last=False):
        both = None if last else load_query(n + 1)
        row_max = mbuf[slot][:, 0:1]
        best = None
        total = jnp.zeros((ROWS, 2 * HEAD), F32)
        for c in range(chunks):
            if not last:
                best = score(both, c, 1 - slot, best)
            total += blend(slot, c, row_max)
        if not last:
            keep_max(1 - slot, best)
        finish(2 * n, total)

    def gather_step(n, c):
        kt = ktbuf[:, keys_of(c)]
        scores = jnp.dot(load_query(n), jnp.concatenate([kt, kt], axis=0), preferred_element_type=F32)
        best = scores[:, 0:128]
        for part in range(1, KEY_CHUNK // 128):
            best = jnp.maximum(best, scores[:, part * 128 : (part + 1) * 128])
        row_max = jnp.max(best, axis=1, keepdims=True)
        if c > 0:
            before = mbuf[n][:, 0:1]
            row_max = jnp.maximum(before, row_max)
        weights = jnp.exp2(scores - row_max).astype(BF16)
        values = kvbuf[slice(c * NY, (c + 1) * NY), 1].reshape(KEY_CHUNK, HEAD)
        total = jnp.dot(weights, jnp.concatenate([values, ones], axis=1), preferred_element_type=F32)
        if c > 0:
            total += acc[n] * jnp.exp2(before - row_max)
        acc[n] = total
        mbuf[n] = jnp.broadcast_to(row_max, (ROWS, 128))

    with jax.named_scope("keys"):
        for j in range(NY):
            if j == OWN:
                own_query.wait()
            else:
                q_copy(j).wait_recv()
        for c in range(chunks):
            for j in range(c * NY, (c + 1) * NY):
                if j == OWN:
                    own_codes.wait()
                else:
                    kv_copy(j).wait_recv()
                ktbuf[:, j * TOK : (j + 1) * TOK] = kvbuf[j, 0].T
            for n in range(2):
                gather_step(n, c)
        for n in range(2):
            finish(2 * n, acc[n])
        for i in range(NY - 1):
            y_copy(0, i).start()

    with jax.named_scope("first"):
        q_copy(NY).wait_recv()
        q_copy(NY + 1).wait_recv()
        both = load_query(2)
        best = None
        for c in range(chunks):
            best = score(both, c, 0, best)
        keep_max(0, best)

    def one_group(g, last=False):
        with jax.named_scope("attend"):
            q_copy(g * NY + 2).wait_recv()
            q_copy(g * NY + 3).wait_recv()
            block(2 * g, 0)
            y_copy(g, 0).start()
            y_copy(g, 1).start()
            if not last:
                q_copy(g * NY + 4).wait_recv()
                q_copy(g * NY + 5).wait_recv()
            block(2 * g + 1, 1, last)
            y_copy(g, 2).start()

    def each_group(g, _):
        one_group(g)
        with jax.named_scope("join"):
            join_y(g - 1)

            @pl.when(g > 1)
            def _():
                z_copy(g - 1).start()

        return 0

    lax.fori_loop(1, NZ - 1, each_group, 0)
    one_group(NZ - 1, True)
    join_y(NZ - 2)
    z_copy(NZ - 2).start()

    with jax.named_scope("tail"):
        join_y(NZ - 1)
        z_copy(NZ - 1).start()
        total = zsend[0]
        for g in range(1, NZ):
            z_copy(g).wait_recv()
            total = total + zbuf[g]

        center = total[LAT : LAT + 1] * (1.0 / WIDTH)
        spread = jnp.maximum(total[LAT + 1 : LAT + 2] * (1.0 / WIDTH) - center * center, 0.0)
        inverse = lax.rsqrt(spread + 1e-06)
        rows = lax.broadcasted_iota(jnp.int32, (128, 128), 0)
        stacked = jnp.where(rows == 0, inverse, jnp.where(rows == 1, center * inverse, 0.0)).T
        left = lax.broadcasted_iota(jnp.int32, (LAT, 128), 1) < LAT
        inverse_at = jnp.where(left, stacked[0:LAT, 0:1], stacked[LAT:, 0:1])
        center_at = jnp.where(left, stacked[0:LAT, 1:2], stacked[LAT:, 1:2])
        velocity = (
            inverse_at * total[0:LAT]
            - center_at * total[LAT + 2 : LAT + 3]
            + total[LAT + 3 : LAT + 4]
        )

        @pl.when(tm < TM - 1)
        def _():
            time_copy.wait_recv()

        @pl.when(tm == TM - 1)
        def _():
            later[1] = jnp.zeros((8, 128), F32)

        step = (later[1] - time_now) / 1000.0
        drift = velocity * step[0:1]
        tsend[...] = drift

        def t_copy(k):
            return pltpu.make_async_remote_copy(
                src_ref=tsend,
                dst_ref=tbuf.at[k - 1],
                send_sem=t_send.at[k - 1],
                recv_sem=t_recv.at[k - 1],
                device_id=((tm + k) % TM, me),
                device_id_type=MESH,
            )

        for k in range(1, TM):

            @pl.when(tm + k < TM)
            def _():
                t_copy(k).start()

        lat[0:LAT] = drift

        for k in range(1, TM):

            @pl.when(tm >= k)
            def _():
                t_copy(k).wait_recv()
                lat[0:LAT] += tbuf[k - 1]

        summed = lat[0:LAT]
        lat[LAT : 2 * LAT] = pltpu.roll(summed, LAT, 1)
        even = lat[pl.ds(0, LAT, stride=2)]
        odd = lat[pl.ds(1, LAT, stride=2)]
        out[...] = start_latent[...] + jnp.where(left, even, pltpu.roll(odd, LAT, 1))

    with jax.named_scope("drain"):

        for j in OTHERS:
            kv_copy(j).wait_send()
            q_copy(j).wait_send()

        def drain_group(g, _):
            for i in range(NY - 1):
                y_copy(g, i).wait_send()

            @pl.when(g > 0)
            def _():
                z_copy(g).wait_send()

            return 0

        lax.fori_loop(0, NZ, drain_group, 0)
        for k in range(1, TM):

            @pl.when(tm + k < TM)
            def _():
                t_copy(k).wait_send()

        @pl.when(tm > 0)
        def _():
            time_copy.wait_send()


def body(projected, scale_table, group_index, timesteps, time_weight, head_weight, start_latent):
    codes = projected[0].transpose(1, 0, 2)
    table = scale_table.transpose(1, 0, 2)
    half = FREQ // 2
    values = np.power(np.float64(10000.0), -np.arange(half, dtype=np.float64) / half).astype(np.float32)
    freqs = jnp.asarray(np.repeat(np.concatenate([values, values]), 2)[None, :])
    any_space = pl.BlockSpec(memory_space=pl.ANY)
    vmem = pl.BlockSpec(memory_space=pltpu.VMEM)
    smem = pl.BlockSpec(memory_space=pltpu.SMEM)
    dma = pltpu.SemaphoreType.DMA
    latents = pl.pallas_call(
        kernel,
        name="window",
        out_shape=pltpu.VMEM((LAT, 128), F32),
        in_specs=[any_space, any_space, smem, smem, any_space, any_space, any_space, any_space],
        out_specs=vmem,
        scratch_shapes=[
            pltpu.VMEM((SEQ, TOK, HEAD), BF16),
            pltpu.VMEM((SEQ, 2, TOK, HEAD), BF16),
            pltpu.VMEM((HEAD, KEYS), BF16),
            pltpu.VMEM((2, ROWS, KEYS), F32),
            pltpu.VMEM((2 * HEAD, 256), BF16),
            pltpu.VMEM((FREQ, 2, HEAD), BF16),
            pltpu.VMEM((LAT, HEAD), BF16),
            pltpu.VMEM((8, 128), F32),
            pltpu.VMEM((3, 8, SEQ), F32),
            pltpu.VMEM((1, 2 * FREQ), F32),
            pltpu.VMEM((LAT, 128), F32),
            pltpu.VMEM((2, ROWS, 128), F32),
            pltpu.VMEM((2, ROWS, 2 * HEAD), F32),
            pltpu.VMEM((SEQ, PACK, 128), F32),
            pltpu.VMEM((SEQ, PACK, 128), F32),
            pltpu.VMEM((NZ, PACK, 128), F32),
            pltpu.VMEM((NZ, PACK, 128), F32),
            pltpu.VMEM((LAT, 128), F32),
            pltpu.VMEM((TM - 1, LAT, 128), F32),
            pltpu.VMEM((2, 8, 128), F32),
            pltpu.VMEM((2 * LAT, 128), F32),
            dma((SEQ,)),
            dma((SEQ,)),
            dma((SEQ,)),
            dma((SEQ,)),
            dma((SEQ,)),
            dma((SEQ,)),
            dma((NZ,)),
            dma((NZ,)),
            dma((TM - 1,)),
            dma((TM - 1,)),
            dma((9,)),
        ],
        compiler_params=pltpu.CompilerParams(
            collective_id=0, has_side_effects=True, vmem_limit_bytes=60 << 20
        ),
    )(codes, table, group_index, timesteps, freqs, time_weight, head_weight, start_latent)
    return latents[None]


def solution(mesh):
    placed = (P("tm", "seq", None, None), P(), P("tm"), P("tm"), P(), P(), P("seq", None))
    return jax.shard_map(
        body, mesh=mesh, in_specs=placed, out_specs=P("tm", "seq", None), check_vma=False
    )
```

```python
import functools
import math

import jax
import jax.numpy as jnp
import numpy as np
from jax import lax
from jax.experimental import pallas as pl
from jax.experimental.pallas import tpu as pltpu
from jax.sharding import PartitionSpec as P

MESH = pl.DeviceIdType.MESH
F32 = jnp.float32
BF16 = jnp.bfloat16

NY, NZ, TM = 4, 8, 8
SEQ = NY * NZ
TOK = 128
HEAD = 128
LAT = 64
KEYS = SEQ * TOK
WIDTH = SEQ * HEAD
FREQ = 256
ROWS = 256
KEY_CHUNK = 512
PACK = 72


def group_dz(g):
    odd = g % 2
    return (odd * ((g + 1) // 2) - (1 - odd) * (g // 2)) % NZ


def group_dy(i):
    return (i + 1) % NY


OWN = NY - 1
OTHERS = [j for j in range(SEQ) if j != OWN]


def kernel(
    proj,
    table_hbm,
    group_index,
    timesteps,
    freqs_hbm,
    time_weight,
    head_weight,
    latent_hbm,
    out,
    qbuf,
    kvbuf,
    ktbuf,
    sbuf,
    wblk,
    tw,
    hw,
    consts,
    scale_table,
    freqs,
    start_latent,
    mbuf,
    acc,
    pbuf,
    ybuf,
    zsend,
    zbuf,
    tsend,
    tbuf,
    later,
    lat,
    kv_send,
    kv_recv,
    q_send,
    q_recv,
    y_send,
    y_recv,
    z_send,
    z_recv,
    t_send,
    t_recv,
    misc,
):
    tm = lax.axis_index("tm")
    me = lax.axis_index("seq")
    my, mz = me // NZ, me % NZ

    def seq_at(dy, dz):
        return ((my + dy + NY) % NY) * NZ + (mz + dz + NZ) % NZ

    def peer(dy, dz):
        return (tm, seq_at(dy, dz))

    cols = pl.ds(pl.multiple_of(me * HEAD, HEAD), HEAD)
    own_codes = pltpu.make_async_copy(proj.at[1:3, :, cols], kvbuf.at[OWN], misc.at[0])
    own_query = pltpu.make_async_copy(proj.at[0, :, cols], qbuf.at[OWN], misc.at[1])
    get_table = pltpu.make_async_copy(table_hbm, scale_table, misc.at[6])
    get_freqs = pltpu.make_async_copy(freqs_hbm, freqs, misc.at[7])
    get_latent = pltpu.make_async_copy(latent_hbm, start_latent, misc.at[8])
    get_table.start()
    get_freqs.start()
    get_latent.start()
    get_tw = pltpu.make_async_copy(time_weight.at[:, :, cols], tw, misc.at[2])
    get_hw = pltpu.make_async_copy(head_weight.at[:, cols], hw, misc.at[3])
    own_codes.start()
    own_query.start()
    get_tw.start()
    get_hw.start()

    barrier = pltpu.get_barrier_semaphore()

    def greet(o, _):
        pl.semaphore_signal(barrier, inc=1, device_id=(tm, (me + o) % SEQ), device_id_type=MESH)
        return 0

    def greet_tm(o, _):
        pl.semaphore_signal(barrier, inc=1, device_id=((tm + o) % TM, me), device_id_type=MESH)
        return 0

    with jax.named_scope("barrier"):
        lax.fori_loop(1, SEQ, greet, 0)
        lax.fori_loop(1, TM, greet_tm, 0)
        pl.semaphore_wait(barrier, SEQ + TM - 2)

    def kv_copy(j):
        g, i = j // NY, j % NY
        to = seq_at(-group_dy(i), -group_dz(g))
        lanes = pl.ds(pl.multiple_of(to * HEAD, HEAD), HEAD)
        return pltpu.make_async_remote_copy(
            src_ref=proj.at[1:3, :, lanes],
            dst_ref=kvbuf.at[j],
            send_sem=kv_send.at[j],
            recv_sem=kv_recv.at[j],
            device_id=(tm, to),
            device_id_type=MESH,
        )

    def q_copy(j):
        g, i = j // NY, j % NY
        to = seq_at(-group_dy(i), -group_dz(g))
        lanes = pl.ds(pl.multiple_of(to * HEAD, HEAD), HEAD)
        return pltpu.make_async_remote_copy(
            src_ref=proj.at[0, :, lanes],
            dst_ref=qbuf.at[j],
            send_sem=q_send.at[j],
            recv_sem=q_recv.at[j],
            device_id=(tm, to),
            device_id_type=MESH,
        )

    with jax.named_scope("send"):
        for j in OTHERS:
            if j < NY:
                q_copy(j).start()
        for j in OTHERS:
            kv_copy(j).start()
        for j in OTHERS:
            if j >= NY:
                q_copy(j).start()

    time_copy = pltpu.make_async_remote_copy(
        src_ref=later.at[0],
        dst_ref=later.at[1],
        send_sem=misc.at[4],
        recv_sem=misc.at[5],
        device_id=((tm + TM - 1) % TM, me),
        device_id_type=MESH,
    )
    time_now = jnp.full((8, 128), timesteps[0], jnp.int32).astype(F32)
    later[0] = time_now

    @pl.when(tm > 0)
    def _():
        time_copy.start()

    with jax.named_scope("constants"):
        get_table.wait()
        get_freqs.wait()
        get_latent.wait()
        row = lax.broadcasted_iota(jnp.int32, (8, 128), 0)
        head_lane = lax.broadcasted_iota(jnp.int32, (8, SEQ), 1)
        group_row = lax.broadcasted_iota(jnp.int32, (8, SEQ), 0)
        chosen = (head_lane == me) & (group_row == group_index[0])

        def pick(k):
            kept = jnp.where(chosen, scale_table[k], 0.0)
            return jnp.sum(jnp.sum(kept, axis=1, keepdims=True), axis=0, keepdims=True)

        factor = pick(0) * pick(1) / math.sqrt(HEAD)
        score_scale = factor * math.log2(math.e)
        value_scale = pick(2)

        angles = time_now[0:1, 0:1] * freqs[...]
        wide_lane = lax.broadcasted_iota(jnp.int32, (8, 2 * FREQ), 1)
        wide_row = lax.broadcasted_iota(jnp.int32, (8, 2 * FREQ), 0)
        waves = jnp.where(wide_lane < FREQ, jnp.cos(angles), jnp.sin(angles))
        waves = jnp.where(wide_lane % 2 == wide_row, waves, 0.0).astype(BF16)
        get_tw.wait()
        get_hw.wait()
        modulation = jnp.dot(waves, tw[...].reshape(2 * FREQ, HEAD), preferred_element_type=F32)
        shift, scale = modulation[0:1], modulation[1:2]
        weight = hw[...].astype(F32)
        weight = jnp.concatenate([weight, weight], axis=0)
        scaled = (weight * (1.0 + scale)).T
        shifted = jnp.sum((weight * shift).T, axis=0, keepdims=True)
        high = scaled.astype(BF16)
        low = (scaled - high.astype(F32)).astype(BF16)
        left = lax.broadcasted_iota(jnp.int32, (HEAD, 128), 1) < LAT
        zero = jnp.zeros_like(high)
        wblk[0:HEAD, 0:128] = jnp.where(left, high, zero)
        wblk[0:HEAD, 128:256] = jnp.where(left, low, zero)
        wblk[HEAD : 2 * HEAD, 0:128] = jnp.where(left, zero, high)
        wblk[HEAD : 2 * HEAD, 128:256] = jnp.where(left, zero, low)
        summed = jnp.sum(high.astype(F32) + low.astype(F32), axis=0, keepdims=True)
        consts[...] = jnp.where(row == 2, summed, jnp.where(row == 3, shifted, 0.0))


    def y_copy(g, i):
        return pltpu.make_async_remote_copy(
            src_ref=pbuf.at[g * NY + i],
            dst_ref=ybuf.at[g * NY + i],
            send_sem=y_send.at[g * NY + i],
            recv_sem=y_recv.at[g * NY + i],
            device_id=peer(group_dy(i), 0),
            device_id_type=MESH,
        )

    def z_copy(g):
        return pltpu.make_async_remote_copy(
            src_ref=zsend.at[g],
            dst_ref=zbuf.at[g],
            send_sem=z_send.at[g],
            recv_sem=z_recv.at[g],
            device_id=peer(0, group_dz(g)),
            device_id_type=MESH,
        )

    def join_y(g):
        total = pbuf[g * NY + NY - 1]
        for i in range(NY - 1):
            y_copy(g, i).wait_recv()
            total = total + ybuf[g * NY + i]
        zsend[g] = total

    keys_of = lambda c: slice(c * KEY_CHUNK, (c + 1) * KEY_CHUNK)
    chunks = KEYS // KEY_CHUNK
    ones = jnp.ones((KEY_CHUNK, 128), BF16)
    stat_row = lax.broadcasted_iota(jnp.int32, (16, 3 * HEAD), 0)
    stat_lane = lax.broadcasted_iota(jnp.int32, (16, 3 * HEAD), 1)
    picker = jnp.where(
        ((stat_row == 0) & (stat_lane < HEAD)) | ((stat_row == 1) & (stat_lane >= HEAD)), 1.0, 0.0
    ).astype(BF16)

    def load_query(n):
        query = qbuf[pl.ds(2 * n, 2)].reshape(ROWS, HEAD).astype(F32) * score_scale
        high = query.astype(BF16)
        low = (query - high.astype(F32)).astype(BF16)
        return jnp.concatenate([high, low], axis=1)

    def score(both, c, slot, best):
        kt = ktbuf[:, keys_of(c)]
        scores = jnp.dot(both, jnp.concatenate([kt, kt], axis=0), preferred_element_type=F32)
        sbuf[slot, :, keys_of(c)] = scores
        for part in range(KEY_CHUNK // 128):
            piece = scores[:, part * 128 : (part + 1) * 128]
            best = piece if best is None else jnp.maximum(best, piece)
        return best

    def keep_max(slot, best):
        mbuf[slot] = jnp.broadcast_to(jnp.max(best, axis=1, keepdims=True), (ROWS, 128))

    def blend(slot, c, row_max):
        weights = jnp.exp2(sbuf[slot, :, keys_of(c)] - row_max).astype(BF16)
        slots = slice(c * KEY_CHUNK // TOK, (c + 1) * KEY_CHUNK // TOK)
        values = kvbuf[slots, 1].reshape(KEY_CHUNK, HEAD)
        return jnp.dot(weights, jnp.concatenate([values, ones], axis=1), preferred_element_type=F32)

    def finish(first, total):
        attended = (total[:, :HEAD] * (value_scale / total[:, HEAD:])).astype(BF16)
        pairs = [
            jnp.concatenate([attended[k * TOK : k * TOK + LAT], attended[k * TOK + LAT : (k + 1) * TOK]], axis=1)
            for k in range(2)
        ]
        partial = jnp.dot(jnp.concatenate(pairs, axis=0), wblk[...], preferred_element_type=F32)
        partial = partial[:, :128] + partial[:, 128:]
        as_float = attended.astype(F32)
        square = as_float * as_float
        square_high = square.astype(BF16)
        square_low = (square - square_high.astype(F32)).astype(BF16)
        stats = lax.dot_general(
            picker,
            jnp.concatenate([attended, square_high, square_low], axis=1),
            (((1,), (1,)), ((), ())),
            preferred_element_type=F32,
        )[0:8]
        for k in range(2):
            pbuf[first + k, 0:LAT] = partial[k * LAT : (k + 1) * LAT]
            pbuf[first + k, LAT:PACK] = stats[:, k * TOK : (k + 1) * TOK] + consts[...]

    def block(n, slot, last=False):
        both = None if last else load_query(n + 1)
        row_max = mbuf[slot][:, 0:1]
        best = None
        total = jnp.zeros((ROWS, 2 * HEAD), F32)
        for c in range(chunks):
            if not last:
                best = score(both, c, 1 - slot, best)
            total += blend(slot, c, row_max)
        if not last:
            keep_max(1 - slot, best)
        finish(2 * n, total)

    def gather_step(n, c):
        kt = ktbuf[:, keys_of(c)]
        scores = jnp.dot(load_query(n), jnp.concatenate([kt, kt], axis=0), preferred_element_type=F32)
        best = scores[:, 0:128]
        for part in range(1, KEY_CHUNK // 128):
            best = jnp.maximum(best, scores[:, part * 128 : (part + 1) * 128])
        row_max = jnp.max(best, axis=1, keepdims=True)
        if c > 0:
            before = mbuf[n][:, 0:1]
            row_max = jnp.maximum(before, row_max)
        weights = jnp.exp2(scores - row_max).astype(BF16)
        values = kvbuf[slice(c * NY, (c + 1) * NY), 1].reshape(KEY_CHUNK, HEAD)
        total = jnp.dot(weights, jnp.concatenate([values, ones], axis=1), preferred_element_type=F32)
        if c > 0:
            total += acc[n] * jnp.exp2(before - row_max)
        acc[n] = total
        mbuf[n] = jnp.broadcast_to(row_max, (ROWS, 128))

    with jax.named_scope("keys"):
        for j in range(NY):
            if j == OWN:
                own_query.wait()
            else:
                q_copy(j).wait_recv()
        for c in range(chunks):
            for j in range(c * NY, (c + 1) * NY):
                if j == OWN:
                    own_codes.wait()
                else:
                    kv_copy(j).wait_recv()
                ktbuf[:, j * TOK : (j + 1) * TOK] = kvbuf[j, 0].T
            for n in range(2):
                gather_step(n, c)
        for n in range(2):
            finish(2 * n, acc[n])
        for i in range(NY - 1):
            y_copy(0, i).start()

    with jax.named_scope("first"):
        q_copy(NY).wait_recv()
        q_copy(NY + 1).wait_recv()
        both = load_query(2)
        best = None
        for c in range(chunks):
            best = score(both, c, 0, best)
        keep_max(0, best)

    def one_group(g, last=False):
        with jax.named_scope("attend"):
            q_copy(g * NY + 2).wait_recv()
            q_copy(g * NY + 3).wait_recv()
            block(2 * g, 0)
            y_copy(g, 0).start()
            y_copy(g, 1).start()
            if not last:
                q_copy(g * NY + 4).wait_recv()
                q_copy(g * NY + 5).wait_recv()
            block(2 * g + 1, 1, last)
            y_copy(g, 2).start()

    def each_group(g, _):
        one_group(g)
        with jax.named_scope("join"):
            join_y(g - 1)

            @pl.when(g > 1)
            def _():
                z_copy(g - 1).start()

        return 0

    lax.fori_loop(1, NZ - 1, each_group, 0)
    one_group(NZ - 1, True)
    join_y(NZ - 2)
    z_copy(NZ - 2).start()

    with jax.named_scope("tail"):
        join_y(NZ - 1)
        z_copy(NZ - 1).start()
        for j in OTHERS:
            kv_copy(j).wait_send()
            q_copy(j).wait_send()
        total = zsend[0]
        for g in range(1, NZ):
            z_copy(g).wait_recv()
            total = total + zbuf[g]

        center = total[LAT : LAT + 1] * (1.0 / WIDTH)
        spread = jnp.maximum(total[LAT + 1 : LAT + 2] * (1.0 / WIDTH) - center * center, 0.0)
        inverse = lax.rsqrt(spread + 1e-06)
        rows = lax.broadcasted_iota(jnp.int32, (128, 128), 0)
        stacked = jnp.where(rows == 0, inverse, jnp.where(rows == 1, center * inverse, 0.0)).T
        left = lax.broadcasted_iota(jnp.int32, (LAT, 128), 1) < LAT
        inverse_at = jnp.where(left, stacked[0:LAT, 0:1], stacked[LAT:, 0:1])
        center_at = jnp.where(left, stacked[0:LAT, 1:2], stacked[LAT:, 1:2])
        velocity = (
            inverse_at * total[0:LAT]
            - center_at * total[LAT + 2 : LAT + 3]
            + total[LAT + 3 : LAT + 4]
        )

        @pl.when(tm < TM - 1)
        def _():
            time_copy.wait_recv()

        @pl.when(tm == TM - 1)
        def _():
            later[1] = jnp.zeros((8, 128), F32)

        step = (later[1] - time_now) / 1000.0
        drift = velocity * step[0:1]
        tsend[...] = drift

        def t_copy(k):
            return pltpu.make_async_remote_copy(
                src_ref=tsend,
                dst_ref=tbuf.at[k - 1],
                send_sem=t_send.at[k - 1],
                recv_sem=t_recv.at[k - 1],
                device_id=((tm + k) % TM, me),
                device_id_type=MESH,
            )

        for k in range(1, TM):

            @pl.when(tm + k < TM)
            def _():
                t_copy(k).start()

        def drain_group(g, _):
            for i in range(NY - 1):
                y_copy(g, i).wait_send()

            @pl.when(g > 0)
            def _():
                z_copy(g).wait_send()

            return 0

        lax.fori_loop(0, NZ, drain_group, 0)
        lat[0:LAT] = drift

        for k in range(1, TM):

            @pl.when(tm >= k)
            def _():
                t_copy(k).wait_recv()
                lat[0:LAT] += tbuf[k - 1]

        summed = lat[0:LAT]
        lat[LAT : 2 * LAT] = pltpu.roll(summed, LAT, 1)
        even = lat[pl.ds(0, LAT, stride=2)]
        odd = lat[pl.ds(1, LAT, stride=2)]
        out[...] = start_latent[...] + jnp.where(left, even, pltpu.roll(odd, LAT, 1))

    with jax.named_scope("drain"):


        for k in range(1, TM):

            @pl.when(tm + k < TM)
            def _():
                t_copy(k).wait_send()

        @pl.when(tm > 0)
        def _():
            time_copy.wait_send()


def body(projected, scale_table, group_index, timesteps, time_weight, head_weight, start_latent):
    codes = projected[0].transpose(1, 0, 2)
    table = scale_table.transpose(1, 0, 2)
    half = FREQ // 2
    values = np.power(np.float64(10000.0), -np.arange(half, dtype=np.float64) / half).astype(np.float32)
    freqs = jnp.asarray(np.repeat(np.concatenate([values, values]), 2)[None, :])
    any_space = pl.BlockSpec(memory_space=pl.ANY)
    vmem = pl.BlockSpec(memory_space=pltpu.VMEM)
    smem = pl.BlockSpec(memory_space=pltpu.SMEM)
    dma = pltpu.SemaphoreType.DMA
    latents = pl.pallas_call(
        kernel,
        name="window",
        out_shape=pltpu.VMEM((LAT, 128), F32),
        in_specs=[any_space, any_space, smem, smem, any_space, any_space, any_space, any_space],
        out_specs=vmem,
        scratch_shapes=[
            pltpu.VMEM((SEQ, TOK, HEAD), BF16),
            pltpu.VMEM((SEQ, 2, TOK, HEAD), BF16),
            pltpu.VMEM((HEAD, KEYS), BF16),
            pltpu.VMEM((2, ROWS, KEYS), F32),
            pltpu.VMEM((2 * HEAD, 256), BF16),
            pltpu.VMEM((FREQ, 2, HEAD), BF16),
            pltpu.VMEM((LAT, HEAD), BF16),
            pltpu.VMEM((8, 128), F32),
            pltpu.VMEM((3, 8, SEQ), F32),
            pltpu.VMEM((1, 2 * FREQ), F32),
            pltpu.VMEM((LAT, 128), F32),
            pltpu.VMEM((2, ROWS, 128), F32),
            pltpu.VMEM((2, ROWS, 2 * HEAD), F32),
            pltpu.VMEM((SEQ, PACK, 128), F32),
            pltpu.VMEM((SEQ, PACK, 128), F32),
            pltpu.VMEM((NZ, PACK, 128), F32),
            pltpu.VMEM((NZ, PACK, 128), F32),
            pltpu.VMEM((LAT, 128), F32),
            pltpu.VMEM((TM - 1, LAT, 128), F32),
            pltpu.VMEM((2, 8, 128), F32),
            pltpu.VMEM((2 * LAT, 128), F32),
            dma((SEQ,)),
            dma((SEQ,)),
            dma((SEQ,)),
            dma((SEQ,)),
            dma((SEQ,)),
            dma((SEQ,)),
            dma((NZ,)),
            dma((NZ,)),
            dma((TM - 1,)),
            dma((TM - 1,)),
            dma((9,)),
        ],
        compiler_params=pltpu.CompilerParams(
            collective_id=0, has_side_effects=True, vmem_limit_bytes=60 << 20
        ),
    )(codes, table, group_index, timesteps, freqs, time_weight, head_weight, start_latent)
    return latents[None]


def solution(mesh):
    placed = (P("tm", "seq", None, None), P(), P("tm"), P("tm"), P(), P(), P("seq", None))
    return jax.shard_map(
        body, mesh=mesh, in_specs=placed, out_specs=P("tm", "seq", None), check_vma=False
    )
```
